32 devices in a mesh: groups: 2 (over y), corpus: 4 (over z), layer: 4 (over x, core).
Axes of the slice: x: 2, y: 2, z: 4, core: 2. Of those that a mesh axis runs over, the one named last changes fastest.
Arguments:
- query_acts: bfloat16 [64, 4, 16, 4096], P(('groups', 'corpus'), 'layer'), parts along dimension 0, may hold values from -6 to 6
- query_outgrads: bfloat16 [64, 4, 16, 4096], P(('groups', 'corpus'), 'layer'), parts along dimension 0, may hold values from -6 to 6
- in_project: bfloat16 [4, 64, 4096], P('layer', None, 'corpus'), may hold values from -0.09375 to 0.09375
- out_project: bfloat16 [4, 64, 4096], P('layer', None, 'corpus'), may hold values from -0.09375 to 0.09375
- in_basis: float32 [4, 64, 64], P('layer'), may hold values from -0.75 to 0.75
- out_basis: float32 [4, 64, 64], P('layer'), may hold values from -0.75 to 0.75
- eig_values: float32 [4, 4096], P('layer'), may hold values from 0.05 to 5
- train_grads: bfloat16 [2560, 4, 4096], P(('groups', 'corpus'), 'layer'), parts along dimension 0, may hold values from -0.099609375 to 0.099609375
Outputs:
- scores: float32 [2560, 32], P(('groups', 'corpus', 'layer')), parts along dimension 0
The draws below stay inside these ranges and needn't reach their ends.
There are 2 independent parts, one for each index of `groups`. The reference program is written for one: setup_inputs(seed, part) draws one part's arguments, and reference() takes and returns one part's arrays. A program takes and returns all parts, laid end to end along the dimension named above; an argument that names none is the same for every part. Nothing has to cross between parts.
All inputs are finite; a program needn't handle non-finite values.
Results may differ from the reference program's by a relative error of at most 0.0059.
Values may be sent and summed in bfloat16 or wider, within the bound.
No kernel may reach another device: no remote copies, remote signals or barrier semaphores. Data moves between devices by JAX's collectives and lax.ppermute only.
A program may use at most 64 MiB of HBM per device.

```python
import math
import jax
import jax.numpy as jnp
from jax import lax

D = 4096
RANK = 64
SEQ = 16
LAYERS = 4
QUERIES = 32
ROWS = 1280


def block_levels(own_key, shape, shards, low, top_value):
    def one(axis_at, blocks):
        heights = jax.random.uniform(jax.random.fold_in(jax.random.fold_in(own_key, 6), axis_at), (blocks,), jnp.float32, low / len(shards), top_value / len(shards))
        return jnp.repeat(jnp.exp(heights), shape[axis_at] // blocks).reshape((-1,) + (1,) * (len(shape) - axis_at - 1))

    loudness = one(*shards[0])
    for cut in shards[1:]:
        loudness = loudness * one(*cut)
    return loudness


def centred(own_key, dims, deviation, reach, split=(), kind=jnp.bfloat16):
    entries = deviation * jax.random.normal(own_key, dims, jnp.float32)
    if split:
        entries = entries * block_levels(own_key, dims, split, -0.22, 0.18)
    return jnp.clip(entries, -reach, reach).astype(kind)


def setup_inputs(seed: int = 0, part: int = 0) -> dict:
    streams_of = jax.random.split(jax.random.key(seed), 9)
    part_splits = jax.random.split(jax.random.fold_in(streams_of[8], part), 9)
    return {
        "query_acts": centred(part_splits[0], (QUERIES, LAYERS, SEQ, D), 1.0, 6.0, ((0, 4), (1, 4))),
        "query_outgrads": centred(part_splits[1], (QUERIES, LAYERS, SEQ, D), 1.0, 6.0, ((0, 4), (1, 4))),
        "in_project": centred(streams_of[2], (LAYERS, RANK, D), D ** -0.5, 0.09375, ((0, 4), (2, 4))),
        "out_project": centred(streams_of[3], (LAYERS, RANK, D), D ** -0.5, 0.09375, ((0, 4), (2, 4))),
        "in_basis": centred(streams_of[4], (LAYERS, RANK, RANK), RANK ** -0.5, 0.75, ((0, 4),), jnp.float32),
        "out_basis": centred(streams_of[5], (LAYERS, RANK, RANK), RANK ** -0.5, 0.75, ((0, 4),), jnp.float32),
        "eig_values": jnp.clip(jnp.exp(math.log(5.0) - 4.6051702 * jax.random.uniform(streams_of[6], (LAYERS, RANK * RANK), jnp.float32) ** block_levels(streams_of[6], (LAYERS, RANK * RANK), ((0, 4),), -0.2, 0.2)), 0.05, 5.0),
        "train_grads": centred(part_splits[7], (ROWS, LAYERS, RANK * RANK), 0.015625, 0.099609375, ((0, 4), (1, 4))),
    }


damping = 0.1


def condition(grads, out_basis, in_basis, inverse):
    count, layers, width = grads.shape
    rank = out_basis.shape[-1]
    highest = lax.Precision.HIGHEST
    square = grads.astype(jnp.float32).reshape(count, layers, rank, rank)
    turned = jnp.einsum('lab,nlad->nlbd', out_basis, square, precision=highest)
    turned = jnp.einsum('nlbd,ldc->nlbc', turned, in_basis, precision=highest)
    scaled = turned * inverse.reshape(1, layers, rank, rank)
    back = jnp.einsum('lab,nlbc->nlac', out_basis, scaled, precision=highest)
    back = jnp.einsum('nlac,ldc->nlad', back, in_basis, precision=highest)
    return back.reshape(count, layers, width).astype(jnp.bfloat16)


def reference(query_acts, query_outgrads, in_project, out_project, in_basis, out_basis, eig_values, train_grads):
    in_side = jnp.einsum('qlsd,lrd->qlsr', query_acts.astype(jnp.float32), in_project.astype(jnp.float32)).astype(jnp.bfloat16)
    out_side = jnp.einsum('qlsd,lrd->qlsr', query_outgrads.astype(jnp.float32), out_project.astype(jnp.float32)).astype(jnp.bfloat16)
    projected = jnp.einsum('qlsa,qlsc->qlac', out_side.astype(jnp.float32), in_side.astype(jnp.float32)) / SEQ
    projected = projected.astype(jnp.bfloat16).reshape(QUERIES, LAYERS, RANK * RANK)
    inverse = 1.0 / (eig_values + damping)
    conditioned = condition(projected, out_basis, in_basis, inverse)
    scores = jnp.zeros((ROWS, QUERIES), jnp.float32)
    for layer_index in range(LAYERS):
        scores = scores + jnp.dot(train_grads[:, layer_index], conditioned[:, layer_index].T, preferred_element_type=jnp.float32)
    return scores
```

```python
import functools

import jax
import jax.numpy as jnp
from jax import lax
from jax.experimental import pallas as pl
from jax.experimental.pallas import tpu as pltpu
from jax.sharding import PartitionSpec as P

damping = 0.1
f32 = jnp.float32
bf16 = jnp.bfloat16
lanes = 256
nt = (((1,), (1,)), ((), ()))
tn = (((0,), (0,)), ((), ()))
vmem = pl.BlockSpec(memory_space=pltpu.VMEM)


def dot(a, b, dims=(((1,), (0,)), ((), ()))):
    return lax.dot_general(a, b, dims, preferred_element_type=f32)


def split(x):
    high = x.astype(bf16)
    return high, (x - high.astype(f32)).astype(bf16)


def tiled_diagonal(x, blocks):
    n = x.shape[0]
    wide = jnp.concatenate([x] * blocks, axis=1)
    tall = jnp.concatenate([wide] * blocks, axis=0)
    row = lax.broadcasted_iota(jnp.int32, tall.shape, 0) // n
    column = lax.broadcasted_iota(jnp.int32, tall.shape, 1) // n
    return jnp.where(row == column, tall, 0.0)


def product3(x, high, low):
    x_high, x_low = split(x)
    return dot(x_high, high) + (dot(x_low, high) + dot(x_high, low))


def sides_kernel(steps, acts, outgrads, *refs):
    group = lax.axis_index("groups")
    place = lax.axis_index("corpus")
    pieces, sides = refs[:-1], refs[-1]
    rank = pieces[0].shape[0]
    width = pieces[0].shape[1]
    in_total = jnp.zeros((acts.shape[0], rank), f32)
    out_total = jnp.zeros((acts.shape[0], rank), f32)
    for at, (shift, swapped) in enumerate(steps):
        first, second = pieces[2 * at][...], pieces[2 * at + 1][...]
        if swapped:
            first, second = jnp.where(group == 0, first, second), jnp.where(group == 0, second, first)
        if width == acts.shape[1]:
            columns = slice(None)
        else:
            columns = pl.ds(pl.multiple_of((place ^ shift) * width, 128), width)
        in_total += dot(acts[:, columns], first, nt)
        out_total += dot(outgrads[:, columns], second, nt)
    sides[...] = jnp.concatenate([out_total, in_total], axis=1).astype(bf16)


def scores_kernel(sources, tokens, in_basis, out_basis, eigen, train, *refs):
    blocks, outs, (scratch, rows) = refs[:sources], refs[sources:-2], refs[-2:]
    rank = in_basis.shape[0]
    across = lanes // rank
    here = blocks[0].shape[0] // tokens
    queries = here * sources
    groups = queries // across
    u_in, u_out = in_basis[...], out_basis[...]
    inverse = 1.0 / (eigen[...] + damping)
    inverse = jnp.concatenate([inverse] * across, axis=1)
    out_high, out_low = split(u_out)
    turn = jnp.concatenate([out_high, out_low], axis=0)
    back = jnp.concatenate([out_high, out_low, out_high], axis=1)
    in_high, in_low = split(tiled_diagonal(u_in, across))
    tin_high, tin_low = split(tiled_diagonal(u_in.T, across))
    mask = (
        lax.broadcasted_iota(jnp.int32, (across * tokens, lanes), 0) // tokens
        == lax.broadcasted_iota(jnp.int32, (across * tokens, lanes), 1) // rank
    )
    parts = [[] for _ in range(groups)]
    for group in range(groups):
        for j in range(across):
            query = j * groups + group
            start = query % here * tokens
            parts[group].append(blocks[query // here][start : start + tokens, :])
    turned = []
    for group in range(groups):
        both = jnp.concatenate(parts[group], axis=0)
        out_side = both[:, :rank]
        in_side = jnp.concatenate([both[:, rank:]] * across, axis=1)
        in_side = jnp.where(mask, in_side, jnp.zeros_like(in_side))
        gradient = (dot(out_side, in_side, tn) * (1.0 / tokens)).astype(bf16)
        turned.append(dot(turn, jnp.concatenate([gradient, gradient], axis=0), tn))
    turned = jnp.concatenate(turned, axis=0)
    turned = product3(turned, in_high, in_low)
    scaled = []
    for group in range(groups):
        part = turned[group * rank : (group + 1) * rank] * inverse
        high, low = split(part)
        scaled.append(dot(back, jnp.concatenate([high, high, low], axis=0)))
    scaled = jnp.concatenate(scaled, axis=0)
    conditioned = product3(scaled, tin_high, tin_low)
    for part in range(lanes // 128):
        scratch[part] = conditioned[:, part * 128 : (part + 1) * 128]
    for pair in range(rank // 2):
        for part in range(lanes // 128):
            even = scratch[part, pl.ds(2 * pair, groups, stride=rank), :]
            odd = scratch[part, pl.ds(2 * pair + 1, groups, stride=rank), :]
            columns = slice(2 * pair * rank, 2 * (pair + 1) * rank)
            for half in range(2):
                j = 2 * part + half
                cut = slice(half * rank, (half + 1) * rank)
                rows[j * groups : (j + 1) * groups, columns] = jnp.concatenate(
                    [even[:, cut], odd[:, cut]], axis=1
                )
    result = dot(train[...], rows[...].astype(bf16), nt)
    scored = result.T
    for at, out in enumerate(outs):
        out[...] = scored


def body(
    query_acts,
    query_outgrads,
    in_project,
    out_project,
    in_basis,
    out_basis,
    eig_values,
    train_grads,
):
    queries_here, _, tokens, model = query_acts.shape
    rank, width = in_project.shape[1:]
    places = model // width
    layers = lax.axis_size("layer")
    acts = query_acts.reshape(queries_here * tokens, model)
    outgrads = query_outgrads.reshape(queries_here * tokens, model)
    in_own, out_own = in_project[0], out_project[0]

    def far(x, shift):
        return lax.ppermute(x, "corpus", [(i, i ^ shift) for i in range(places)])

    if places == 4 and lax.axis_size("groups") == 2:
        half = jnp.where(lax.axis_index("groups") == 0, in_own, out_own)
        steps, pieces = [(0, False)], [in_own, out_own]
        for shift in (3, 2):
            got = far(half, shift)
            other = lax.ppermute(got, "groups", [(0, 1), (1, 0)])
            steps.append((shift, True))
            pieces += [got, other]
        steps.append((1, False))
        pieces += [far(in_own, 1), far(out_own, 1)]
    else:
        steps = [(0, False)]
        pieces = [lax.all_gather(x, "corpus", axis=1, tiled=True) for x in (in_own, out_own)]
    sides = pl.pallas_call(
        functools.partial(sides_kernel, steps),
        out_shape=jax.ShapeDtypeStruct((queries_here * tokens, 2 * rank), bf16),
        in_specs=[vmem] * (2 + len(pieces)),
        out_specs=vmem,
        name="sides",
    )(acts, outgrads, *pieces)

    eigen = eig_values.reshape(rank, rank)
    train = train_grads.reshape(train_grads.shape[0], rank * rank)
    rows_here = train.shape[0]
    if places == 4:
        blocks = [sides] + [far(sides, shift) for shift in (1, 2, 3)]
        queries = 4 * queries_here
        scored = pl.pallas_call(
            functools.partial(scores_kernel, 4, tokens),
            out_shape=jax.ShapeDtypeStruct((queries, rows_here), f32),
            in_specs=[vmem] * 8,
            out_specs=vmem,
            scratch_shapes=[
                pltpu.VMEM((lanes // 128, queries * rank * rank // lanes, 128), f32),
                pltpu.VMEM((queries, rank * rank), f32),
            ],
            name="scores",
        )(in_basis[0], out_basis[0], eigen, train, *blocks)
        place = lax.axis_index("corpus")
        scored = scored.reshape(4, queries_here, rows_here)
        scored = jnp.concatenate(
            [lax.dynamic_slice_in_dim(scored, place ^ i, 1, 0) for i in range(4)], axis=0
        ).reshape(queries, rows_here)
    else:
        everything = lax.all_gather(sides, "corpus", axis=0, tiled=True)
        chunk = 32
        queries = everything.shape[0] // tokens
        scored = pl.pallas_call(
            functools.partial(scores_kernel, 1, tokens),
            out_shape=jax.ShapeDtypeStruct((queries, rows_here), f32),
            grid=(queries // chunk,),
            in_specs=[vmem] * 4 + [pl.BlockSpec((chunk * tokens, 2 * rank), lambda i: (i, 0))],
            out_specs=pl.BlockSpec((chunk, rows_here), lambda i: (i, 0)),
            scratch_shapes=[
                pltpu.VMEM((lanes // 128, chunk * rank * rank // lanes, 128), f32),
                pltpu.VMEM((chunk, rank * rank), f32),
            ],
            name="scores",
        )(in_basis[0], out_basis[0], eigen, train, everything)

    rows_out = rows_here // layers
    layer = lax.axis_index("layer")

    def slab(which):
        return lax.dynamic_slice_in_dim(scored, which * rows_out, rows_out, 1)

    total = slab(layer)
    for shift in range(1, layers):
        total += lax.ppermute(slab(layer ^ shift), "layer", [(i, i ^ shift) for i in range(layers)])
    return total.T


def solution(mesh):
    placed = (
        P(("groups", "corpus"), "layer", None, None),
        P(("groups", "corpus"), "layer", None, None),
        P("layer", None, "corpus"),
        P("layer", None, "corpus"),
        P("layer", None, None),
        P("layer", None, None),
        P("layer", None),
        P(("groups", "corpus"), "layer", None),
    )
    return jax.shard_map(
        body,
        mesh=mesh,
        in_specs=placed,
        out_specs=P(("groups", "corpus", "layer"), None),
        check_vma=False,
    )
```

```python
import functools

import jax
import jax.numpy as jnp
from jax import lax
from jax.experimental import pallas as pl
from jax.experimental.pallas import tpu as pltpu
from jax.sharding import PartitionSpec as P

damping = 0.1
f32 = jnp.float32
bf16 = jnp.bfloat16
lanes = 256
nt = (((1,), (1,)), ((), ()))
tn = (((0,), (0,)), ((), ()))
vmem = pl.BlockSpec(memory_space=pltpu.VMEM)
params = pltpu.CompilerParams(vmem_limit_bytes=16 << 20)


def dot(a, b, dims=(((1,), (0,)), ((), ()))):
    return lax.dot_general(a, b, dims, preferred_element_type=f32)


def split(x):
    high = x.astype(bf16)
    return high, (x - high.astype(f32)).astype(bf16)


def tiled_diagonal(x, blocks):
    n = x.shape[0]
    wide = jnp.concatenate([x] * blocks, axis=1)
    tall = jnp.concatenate([wide] * blocks, axis=0)
    row = lax.broadcasted_iota(jnp.int32, tall.shape, 0) // n
    column = lax.broadcasted_iota(jnp.int32, tall.shape, 1) // n
    return jnp.where(row == column, tall, 0.0)


def product3(x, high, low):
    x_high, x_low = split(x)
    return dot(x_high, high) + (dot(x_low, high) + dot(x_high, low))


def sides_kernel(plan, acts, outgrads, *refs):
    total, sides = refs[len(plan) : -1], refs[-1]
    group, place = lax.axis_index("groups"), lax.axis_index("corpus")
    sums = [jnp.zeros((acts.shape[0], sides.shape[1] // 2), f32)] * 2
    for (side, first), piece in zip(plan, refs):
        width = piece.shape[1]
        columns = pl.ds(pl.multiple_of(first(group, place), 128), width)
        inputs = acts if side else outgrads
        sums[side] += dot(inputs[:, columns], piece[...], nt)
    result = jnp.concatenate(sums, axis=1)
    if total:
        result += total[0][...]
    sides[...] = result.astype(sides.dtype)


def scores_kernel(sources, shifts, tokens, in_basis, out_basis, eigen, train, *refs):
    blocks, (scratch, rows, tall) = refs[:sources], refs[-3:]
    layers = lax.axis_size("layer")
    given = refs[sources : -3 - layers]
    outs = refs[-3 - layers : -3]
    rank = in_basis.shape[0]
    across = lanes // rank
    here = blocks[0].shape[0] // tokens
    queries = here * sources
    groups = queries // across
    u_in, u_out = in_basis[...], out_basis[...]
    inverse = 1.0 / (eigen[...] + damping)
    inverse = jnp.concatenate([inverse] * across, axis=1)
    out_high, out_low = split(u_out)
    turn = jnp.concatenate([out_high, out_low], axis=0)
    back = jnp.concatenate([out_high, out_low, out_high], axis=1)
    in_high, in_low = split(tiled_diagonal(u_in, across))
    tin_high, tin_low = split(tiled_diagonal(u_in.T, across))
    mask = (
        lax.broadcasted_iota(jnp.int32, (across * tokens, lanes), 0) // tokens
        == lax.broadcasted_iota(jnp.int32, (across * tokens, lanes), 1) // rank
    )
    parts = [[] for _ in range(groups)]
    for group in range(groups):
        for j in range(across):
            query = j * groups + group
            start = query % here * tokens
            parts[group].append(blocks[query // here][start : start + tokens, :])
    turned = []
    for group in range(groups):
        both = jnp.concatenate(parts[group], axis=0)
        out_side = both[:, :rank]
        in_side = jnp.concatenate([both[:, rank:]] * across, axis=1)
        in_side = jnp.where(mask, in_side, jnp.zeros_like(in_side))
        gradient = (dot(out_side, in_side, tn) * (1.0 / tokens)).astype(bf16)
        turned.append(dot(turn, jnp.concatenate([gradient, gradient], axis=0), tn))
    turned = jnp.concatenate(turned, axis=0)
    turned = product3(turned, in_high, in_low)
    scaled = []
    for group in range(groups):
        part = turned[group * rank : (group + 1) * rank] * inverse
        high, low = split(part)
        scaled.append(dot(back, jnp.concatenate([high, high, low], axis=0)))
    scaled = jnp.concatenate(scaled, axis=0)
    conditioned = product3(scaled, tin_high, tin_low)
    for part in range(lanes // 128):
        scratch[part] = conditioned[:, part * 128 : (part + 1) * 128]
    for pair in range(rank // 2):
        for part in range(lanes // 128):
            even = scratch[part, pl.ds(2 * pair, groups, stride=rank), :]
            odd = scratch[part, pl.ds(2 * pair + 1, groups, stride=rank), :]
            columns = slice(2 * pair * rank, 2 * (pair + 1) * rank)
            for half in range(2):
                j = 2 * part + half
                cut = slice(half * rank, (half + 1) * rank)
                rows[j * groups : (j + 1) * groups, columns] = jnp.concatenate(
                    [even[:, cut], odd[:, cut]], axis=1
                )
    tall[...] = dot(train[...], rows[...].astype(bf16), nt)
    layer, place = lax.axis_index("layer"), lax.axis_index("corpus")
    slab_rows = train.shape[0] // layers
    for shift, out in enumerate(outs):
        slab = tall[pl.ds(pl.multiple_of((layer ^ shift) * slab_rows, 8), slab_rows), :].T
        if shifts is None:
            out[...] = slab
            continue
        out[pl.ds(pl.multiple_of(place * here, 8), here), :] = given[shift][...]
        for at, far in enumerate(shifts):
            to = pl.ds(pl.multiple_of((place ^ far) * here, 8), here)
            out[to, :] = slab[at * here : (at + 1) * here]


def body(
    query_acts,
    query_outgrads,
    in_project,
    out_project,
    in_basis,
    out_basis,
    eig_values,
    train_grads,
):
    queries_here, _, tokens, model = query_acts.shape
    rank, width = in_project.shape[1:]
    places = model // width
    layers = lax.axis_size("layer")
    acts = query_acts.reshape(queries_here * tokens, model)
    outgrads = query_outgrads.reshape(queries_here * tokens, model)
    in_own, out_own = in_project[0], out_project[0]

    def far(x, shift):
        return lax.ppermute(x, "corpus", [(i, i ^ shift) for i in range(places)])

    def mixed(x, shifts):
        pairs = [(g * places + i, g * places + (i ^ shifts[g])) for g in range(2) for i in range(places)]
        return lax.ppermute(x, ("groups", "corpus"), pairs)

    def swapped(x):
        return lax.ppermute(x, "groups", [(0, 1), (1, 0)])

    def sides_call(plan, pieces, total, dtype):
        return pl.pallas_call(
            functools.partial(sides_kernel, plan),
            out_shape=jax.ShapeDtypeStruct((queries_here * tokens, 2 * rank), dtype),
            in_specs=[vmem] * (2 + len(pieces) + len(total)),
            out_specs=vmem,
            compiler_params=params,
            name="sides",
        )(acts, outgrads, *pieces, *total)

    eigen = eig_values.reshape(rank, rank)
    train = train_grads.reshape(train_grads.shape[0], rank * rank)
    rows_out = train.shape[0] // layers

    def scores_call(shifts, blocks, given, chunk):
        queries = sum(x.shape[0] for x in blocks) // tokens + (queries_here if given else 0)
        here = blocks[0].shape[0] // tokens // (chunk or 1)
        count = here * len(blocks)
        out_rows = queries // (chunk or 1)
        if chunk:
            specs = dict(
                grid=(chunk,),
                in_specs=[vmem] * 4 + [pl.BlockSpec((here * tokens, 2 * rank), lambda i: (i, 0))],
                out_specs=[pl.BlockSpec((out_rows, rows_out), lambda i: (i, 0))] * layers,
            )
        else:
            specs = dict(in_specs=[vmem] * (4 + len(blocks) + len(given)), out_specs=[vmem] * layers)
        return pl.pallas_call(
            functools.partial(scores_kernel, len(blocks), shifts, tokens),
            out_shape=[jax.ShapeDtypeStruct((queries, rows_out), f32)] * layers,
            scratch_shapes=[
                pltpu.VMEM((lanes // 128, count * rank * rank // lanes, 128), f32),
                pltpu.VMEM((count, rank * rank), f32),
                pltpu.VMEM((train.shape[0], count), f32),
            ],
            compiler_params=params,
            name="scores",
            **specs,
        )(in_basis[0], out_basis[0], eigen, train, *blocks, *given)

    if places == 4 and lax.axis_size("groups") == 2:
        part = width // 2
        near = mixed(in_own, (3, 1))
        near_out = mixed(out_own, (1, 3))
        cut = far(lax.dynamic_slice_in_dim(out_own, lax.axis_index("groups") * part, part, 1), 2)
        last = far(in_own, 2)
        direct = lambda g, p: (p ^ 2) * width
        first, second = (lambda g, p: (p ^ (3 - 2 * g)) * width), (lambda g, p: (p ^ (1 + 2 * g)) * width)
        mine = lambda g, p: (p ^ 2) * width + g * part
        other = lambda g, p: (p ^ 2) * width + (1 - g) * part
        total = sides_call([(1, lambda g, p: p * width), (0, lambda g, p: p * width)], [in_own, out_own], [], f32)
        near, total, eigen = lax.optimization_barrier((near, total, eigen))
        total = sides_call(
            [(1, first), (0, second), (0, mine), (1, direct)], [near, near_out, cut, last], [total], f32
        )
        sides = sides_call(
            [(1, second), (0, first), (0, other)],
            [swapped(near), swapped(near_out), swapped(cut)],
            [total],
            bf16,
        )
        arrived = [far(sides, shift) for shift in (3, 2, 1)]
        own = scores_call(None, [sides], [], None)
        slabs = scores_call((3, 2, 1), arrived, own, None)
    else:
        pieces = [lax.all_gather(x, "corpus", axis=1, tiled=True) for x in (in_own, out_own)]
        sides = sides_call([(1, lambda g, p: 0), (0, lambda g, p: 0)], pieces, [], bf16)
        everything = lax.all_gather(sides, "corpus", axis=0, tiled=True)
        slabs = scores_call(None, [everything], [], everything.shape[0] // tokens // 32)

    total = slabs[0]
    for shift in range(1, layers):
        total += lax.ppermute(slabs[shift], "layer", [(i, i ^ shift) for i in range(layers)])
    return total.T


def solution(mesh):
    placed = (
        P(("groups", "corpus"), "layer", None, None),
        P(("groups", "corpus"), "layer", None, None),
        P("layer", None, "corpus"),
        P("layer", None, "corpus"),
        P("layer", None, None),
        P("layer", None, None),
        P("layer", None),
        P(("groups", "corpus"), "layer", None),
    )
    return jax.shard_map(
        body,
        mesh=mesh,
        in_specs=placed,
        out_specs=P(("groups", "corpus", "layer"), None),
        check_vma=False,
    )
```

```python
import functools

import jax
import jax.numpy as jnp
from jax import lax
from jax.experimental import pallas as pl
from jax.experimental.pallas import tpu as pltpu
from jax.sharding import PartitionSpec as P

damping = 0.1
f32 = jnp.float32
bf16 = jnp.bfloat16
lanes = 256
nt = (((1,), (1,)), ((), ()))
tn = (((0,), (0,)), ((), ()))
vmem = pl.BlockSpec(memory_space=pltpu.VMEM)
params = pltpu.CompilerParams(vmem_limit_bytes=16 << 20)


def dot(a, b, dims=(((1,), (0,)), ((), ()))):
    return lax.dot_general(a, b, dims, preferred_element_type=f32)


def split(x):
    high = x.astype(bf16)
    return high, (x - high.astype(f32)).astype(bf16)


def tiled_diagonal(x, blocks):
    n = x.shape[0]
    wide = jnp.concatenate([x] * blocks, axis=1)
    tall = jnp.concatenate([wide] * blocks, axis=0)
    row = lax.broadcasted_iota(jnp.int32, tall.shape, 0) // n
    column = lax.broadcasted_iota(jnp.int32, tall.shape, 1) // n
    return jnp.where(row == column, tall, 0.0)


def product3(x, high, low):
    x_high, x_low = split(x)
    return dot(x_high, high) + (dot(x_low, high) + dot(x_high, low))


def sides_kernel(plan, acts, outgrads, *refs):
    total, sides = refs[len(plan) : -1], refs[-1]
    group, place = lax.axis_index("groups"), lax.axis_index("corpus")
    sums = [jnp.zeros((acts.shape[0], sides.shape[1] // 2), f32)] * 2
    for (side, first), piece in zip(plan, refs):
        width = piece.shape[1]
        columns = pl.ds(pl.multiple_of(first(group, place), 128), width)
        inputs = acts if side else outgrads
        sums[side] += dot(inputs[:, columns], piece[...], nt)
    result = jnp.concatenate(sums, axis=1)
    if total:
        result += total[0][...]
    sides[...] = result.astype(sides.dtype)


def prepare_kernel(in_own, out_own, acts, outgrads, in_basis, out_basis, eigen, *refs):
    total, acts_here, outgrads_here, turn, back, turns, inverse = refs[:7]
    in_here, out_here, u_in, u_out, values, spread, sems = refs[7:]
    width = in_own.shape[1]
    pairs = [(in_basis, u_in), (out_basis, u_out), (eigen, values)]
    pairs += [(in_own, in_here), (out_own, out_here), (acts, acts_here), (outgrads, outgrads_here)]
    copies = [pltpu.make_async_copy(a, b, sems.at[i]) for i, (a, b) in enumerate(pairs)]
    for copy in copies:
        copy.start()
    for copy in copies[:3]:
        copy.wait()
    lay_out(u_in, u_out, values, turn, back, turns, inverse, spread)
    for copy in copies[3:]:
        copy.wait()
    columns = pl.ds(pl.multiple_of(lax.axis_index("corpus") * width, 128), width)
    total[...] = jnp.concatenate(
        [dot(outgrads_here[:, columns], out_here[...], nt), dot(acts_here[:, columns], in_here[...], nt)], axis=1
    )


def lay_out(in_basis, out_basis, eigen, turn, back, turns, inverse, spread):
    rank = in_basis.shape[0]
    across = lanes // rank
    for at in range(rank):
        spread[at : at + 1, :] = eigen[:, at * rank : (at + 1) * rank]
    inverse[...] = jnp.concatenate([1.0 / (spread[...] + damping)] * across, axis=1)
    out_high, out_low = split(out_basis[...])
    u_in = in_basis[...]
    in_high, in_low = split(u_in)
    for at, (of_out, of_in) in enumerate(((out_high, in_high), (out_low, in_low))):
        zero = jnp.zeros_like(of_out)
        top = jnp.concatenate([of_out, of_out, zero, zero], axis=1)
        bottom = jnp.concatenate([zero, zero, of_in, of_in], axis=1)
        turn[:, at * lanes : (at + 1) * lanes] = jnp.concatenate([top, bottom], axis=0)
    back[...] = jnp.concatenate([out_high, out_low, out_high], axis=1)
    for at, part in enumerate(split(tiled_diagonal(u_in.T, across))):
        turns[at * lanes : (at + 1) * lanes, :] = part


def scores_kernel(sources, shifts, tokens, turn, back, turns, inverse, train, *refs):
    blocks, (scratch, rows, tall) = refs[:sources], refs[-3:]
    layers = lax.axis_size("layer")
    given = refs[sources : -3 - layers]
    outs = refs[-3 - layers : -3]
    rank = turn.shape[0] // 2
    across = lanes // rank
    here = blocks[0].shape[0] // tokens
    queries = here * sources
    groups = queries // across
    back, inverse = back[...], inverse[...] * (1.0 / tokens)
    mask = (
        lax.broadcasted_iota(jnp.int32, (across * tokens, lanes), 0) // tokens
        == lax.broadcasted_iota(jnp.int32, (across * tokens, lanes), 1) // rank
    )
    parts = []
    for block in blocks:
        both = dot(block[...], turn[...])
        parts.append(split(both[:, :lanes] + both[:, lanes:]))
    scaled = []
    for group in range(groups):
        high, low = [], []
        for j in range(across):
            query = j * groups + group
            start = query % here * tokens
            for kept, part in zip((high, low), parts[query // here]):
                kept.append(part[start : start + tokens])
        high, low = jnp.concatenate(high, axis=0), jnp.concatenate(low, axis=0)
        out_high, out_low = high[:, :rank], low[:, :rank]
        in_high, in_low = (
            jnp.where(mask, jnp.concatenate([x[:, lanes // 2 :]] * 2, axis=1), jnp.zeros(mask.shape, bf16))
            for x in (high, low)
        )
        gradient = dot(
            jnp.concatenate([out_high, out_low, out_high], axis=0),
            jnp.concatenate([in_high, in_high, in_low], axis=0),
            tn,
        )
        high, low = split(gradient * inverse)
        scaled.append(dot(back, jnp.concatenate([high, high, low], axis=0)))
    scaled = jnp.concatenate(scaled, axis=0)
    conditioned = product3(scaled, turns[:lanes, :], turns[lanes:, :])
    for part in range(lanes // 128):
        scratch[part] = conditioned[:, part * 128 : (part + 1) * 128]
    for pair in range(rank // 2):
        for part in range(lanes // 128):
            even = scratch[part, pl.ds(2 * pair, groups, stride=rank), :]
            odd = scratch[part, pl.ds(2 * pair + 1, groups, stride=rank), :]
            columns = slice(2 * pair * rank, 2 * (pair + 1) * rank)
            for half in range(2):
                j = 2 * part + half
                cut = slice(half * rank, (half + 1) * rank)
                rows[j * groups : (j + 1) * groups, columns] = jnp.concatenate(
                    [even[:, cut], odd[:, cut]], axis=1
                )
    conditioned = rows[...].astype(bf16)
    middle = train.shape[0] // 32 * 16
    tall[:middle] = dot(train[:middle], conditioned, nt)
    tall[middle:] = dot(train[middle:], conditioned, nt)
    layer, place = lax.axis_index("layer"), lax.axis_index("corpus")
    slab_rows = train.shape[0] // layers
    for shift, out in enumerate(outs):
        slab = tall[pl.ds(pl.multiple_of((layer ^ shift) * slab_rows, 8), slab_rows), :].T
        if shifts is None:
            out[...] = slab
            continue
        out[pl.ds(pl.multiple_of(place * here, 8), here), :] = given[shift][...]
        for at, far in enumerate(shifts):
            to = pl.ds(pl.multiple_of((place ^ far) * here, 8), here)
            out[to, :] = slab[at * here : (at + 1) * here]


def body(
    query_acts,
    query_outgrads,
    in_project,
    out_project,
    in_basis,
    out_basis,
    eig_values,
    train_grads,
):
    queries_here, _, tokens, model = query_acts.shape
    rank, width = in_project.shape[1:]
    places = model // width
    layers = lax.axis_size("layer")
    acts = query_acts.reshape(queries_here * tokens, model)
    outgrads = query_outgrads.reshape(queries_here * tokens, model)
    in_own, out_own = in_project[0], out_project[0]

    def far(x, shift):
        return lax.ppermute(x, "corpus", [(i, i ^ shift) for i in range(places)])

    def mixed(x, shifts):
        pairs = [(g * places + i, g * places + (i ^ shifts[g])) for g in range(2) for i in range(places)]
        return lax.ppermute(x, ("groups", "corpus"), pairs)

    def swapped(x):
        return lax.ppermute(x, "groups", [(0, 1), (1, 0)])

    def sides_call(plan, pieces, totals, dtype):
        return pl.pallas_call(
            functools.partial(sides_kernel, plan),
            out_shape=jax.ShapeDtypeStruct((queries_here * tokens, 2 * rank), dtype),
            in_specs=[vmem] * (2 + len(pieces) + len(totals)),
            out_specs=vmem,
            compiler_params=params,
            name="sides",
        )(acts, outgrads, *pieces, *totals)

    stay = functools.partial(pltpu.with_memory_space_constraint, memory_space=pltpu.HBM)
    hbm = pl.BlockSpec(memory_space=pltpu.HBM)
    prepared = pl.pallas_call(
        prepare_kernel,
        out_shape=[
            jax.ShapeDtypeStruct((queries_here * tokens, 2 * rank), f32),
            jax.ShapeDtypeStruct(acts.shape, bf16),
            jax.ShapeDtypeStruct(acts.shape, bf16),
            jax.ShapeDtypeStruct((2 * rank, 2 * lanes), bf16),
            jax.ShapeDtypeStruct((rank, 3 * rank), bf16),
            jax.ShapeDtypeStruct((2 * lanes, lanes), bf16),
            jax.ShapeDtypeStruct((rank, lanes), f32),
        ],
        in_specs=[hbm] * 7,
        out_specs=[vmem] * 7,
        scratch_shapes=[
            pltpu.VMEM((rank, width), bf16),
            pltpu.VMEM((rank, width), bf16),
            pltpu.VMEM((rank, rank), f32),
            pltpu.VMEM((rank, rank), f32),
            pltpu.VMEM((1, rank * rank), f32),
            pltpu.VMEM((rank, rank), f32),
            pltpu.SemaphoreType.DMA((7,)),
        ],
        compiler_params=params,
        name="prepare",
    )(*(stay(x) for x in (in_own, out_own, acts, outgrads, in_basis[0], out_basis[0], eig_values)))
    total, acts, outgrads = prepared[:3]
    train = train_grads.reshape(train_grads.shape[0], rank * rank)
    rows_out = train.shape[0] // layers

    def scores_call(shifts, blocks, given, chunk):
        queries = sum(x.shape[0] for x in blocks) // tokens + (queries_here if given else 0)
        here = blocks[0].shape[0] // tokens // (chunk or 1)
        count = here * len(blocks)
        out_rows = queries // (chunk or 1)
        if chunk:
            specs = dict(
                grid=(chunk,),
                in_specs=[vmem] * 5 + [pl.BlockSpec((here * tokens, 2 * rank), lambda i: (i, 0))],
                out_specs=[pl.BlockSpec((out_rows, rows_out), lambda i: (i, 0))] * layers,
            )
        else:
            specs = dict(in_specs=[vmem] * (5 + len(blocks) + len(given)), out_specs=[vmem] * layers)
        return pl.pallas_call(
            functools.partial(scores_kernel, len(blocks), shifts, tokens),
            out_shape=[jax.ShapeDtypeStruct((queries, rows_out), f32)] * layers,
            scratch_shapes=[
                pltpu.VMEM((lanes // 128, count * rank * rank // lanes, 128), f32),
                pltpu.VMEM((count, rank * rank), f32),
                pltpu.VMEM((train.shape[0], count), f32),
            ],
            compiler_params=params,
            name="scores",
            **specs,
        )(*prepared[3:], train, *blocks, *given)

    if places == 4 and lax.axis_size("groups") == 2:
        part = width // 2
        near = mixed(in_own, (3, 1))
        near_out = mixed(out_own, (1, 3))
        last, last_out = far(in_own, 2), far(out_own, 2)
        near, total = lax.optimization_barrier((near, total))
        direct = lambda g, p: (p ^ 2) * width
        first = lambda g, p: (p ^ jnp.where(g == 0, 3, 1)) * width
        second = lambda g, p: (p ^ jnp.where(g == 0, 1, 3)) * width
        mine = lambda g, p: (p ^ 2) * width + g * part
        other = lambda g, p: (p ^ 2) * width + (1 - g) * part
        total = sides_call([(1, first), (0, second)], [near, near_out], [total], f32)
        sides = sides_call([(1, second), (0, first), (1, direct), (0, direct)], [swapped(near), swapped(near_out), last, last_out], [total], bf16)
        arrived = [far(sides, shift) for shift in (3, 2, 1)]
        own = scores_call(None, [sides], [], None)
        slabs = scores_call((3, 2, 1), arrived, own, None)
    else:
        pieces = [lax.all_gather(x, "corpus", axis=1, tiled=True) for x in (in_own, out_own)]
        sides = sides_call([(1, lambda g, p: 0), (0, lambda g, p: 0)], pieces, [], bf16)
        everything = lax.all_gather(sides, "corpus", axis=0, tiled=True)
        slabs = scores_call(None, [everything], [], everything.shape[0] // tokens // 32)

    total = slabs[0]
    for shift in range(1, layers):
        total += lax.ppermute(slabs[shift], "layer", [(i, i ^ shift) for i in range(layers)])
    return total.T


def solution(mesh):
    placed = (
        P(("groups", "corpus"), "layer", None, None),
        P(("groups", "corpus"), "layer", None, None),
        P("layer", None, "corpus"),
        P("layer", None, "corpus"),
        P("layer", None, None),
        P("layer", None, None),
        P("layer", None),
        P(("groups", "corpus"), "layer", None),
    )
    return jax.shard_map(
        body,
        mesh=mesh,
        in_specs=placed,
        out_specs=P(("groups", "corpus", "layer"), None),
        check_vma=False,
    )
```

```python
import functools

import jax
import jax.numpy as jnp
from jax import lax
from jax.experimental import pallas as pl
from jax.experimental.pallas import tpu as pltpu
from jax.sharding import PartitionSpec as P

damping = 0.1
f32 = jnp.float32
bf16 = jnp.bfloat16
lanes = 256
nt = (((1,), (1,)), ((), ()))
tn = (((0,), (0,)), ((), ()))
vmem = pl.BlockSpec(memory_space=pltpu.VMEM)
params = pltpu.CompilerParams(vmem_limit_bytes=16 << 20)


def dot(a, b, dims=(((1,), (0,)), ((), ()))):
    return lax.dot_general(a, b, dims, preferred_element_type=f32)


def split(x):
    high = x.astype(bf16)
    return high, (x - high.astype(f32)).astype(bf16)


def tiled_diagonal(x, blocks):
    n = x.shape[0]
    wide = jnp.concatenate([x] * blocks, axis=1)
    tall = jnp.concatenate([wide] * blocks, axis=0)
    row = lax.broadcasted_iota(jnp.int32, tall.shape, 0) // n
    column = lax.broadcasted_iota(jnp.int32, tall.shape, 1) // n
    return jnp.where(row == column, tall, 0.0)


def product3(x, high, low):
    x_high, x_low = split(x)
    return dot(x_high, high) + (dot(x_low, high) + dot(x_high, low))


def sides_kernel(plan, acts, outgrads, *refs):
    total, sides = refs[len(plan) : -1], refs[-1]
    group, place = lax.axis_index("groups"), lax.axis_index("corpus")
    sums = [jnp.zeros((acts.shape[0], sides.shape[1] // 2), f32)] * 2
    for (side, first), piece in zip(plan, refs):
        width = piece.shape[1]
        columns = pl.ds(pl.multiple_of(first(group, place), 128), width)
        inputs = acts if side else outgrads
        sums[side] += dot(inputs[:, columns], piece[...], nt)
    result = jnp.concatenate(sums, axis=1)
    if total:
        result += total[0][...]
    sides[...] = result.astype(sides.dtype)


def prepare_kernel(in_own, out_own, acts, outgrads, in_basis, out_basis, eigen, *refs):
    total, acts_here, outgrads_here, turn, back, turns, inverse = refs[:7]
    in_here, out_here, u_in, u_out, values, spread, sems = refs[7:]
    width = in_own.shape[1]
    pairs = [(in_basis, u_in), (out_basis, u_out), (eigen, values)]
    pairs += [(in_own, in_here), (out_own, out_here), (acts, acts_here), (outgrads, outgrads_here)]
    copies = [pltpu.make_async_copy(a, b, sems.at[i]) for i, (a, b) in enumerate(pairs)]
    for copy in copies:
        copy.start()
    for copy in copies[:3]:
        copy.wait()
    lay_out(u_in, u_out, values, turn, back, turns, inverse, spread)
    for copy in copies[3:]:
        copy.wait()
    columns = pl.ds(pl.multiple_of(lax.axis_index("corpus") * width, 128), width)
    total[...] = jnp.concatenate(
        [dot(outgrads_here[:, columns], out_here[...], nt), dot(acts_here[:, columns], in_here[...], nt)], axis=1
    )


def lay_out(in_basis, out_basis, eigen, turn, back, turns, inverse, spread):
    rank = in_basis.shape[0]
    across = lanes // rank
    for at in range(rank):
        spread[at : at + 1, :] = eigen[:, at * rank : (at + 1) * rank]
    inverse[...] = jnp.concatenate([1.0 / (spread[...] + damping)] * across, axis=1)
    out_high, out_low = split(out_basis[...])
    u_in = in_basis[...]
    in_high, in_low = split(u_in)
    for at, (of_out, of_in) in enumerate(((out_high, in_high), (out_low, in_low))):
        zero = jnp.zeros_like(of_out)
        top = jnp.concatenate([of_out, of_out, zero, zero], axis=1)
        bottom = jnp.concatenate([zero, zero, of_in, of_in], axis=1)
        turn[:, at * lanes : (at + 1) * lanes] = jnp.concatenate([top, bottom], axis=0)
    back[...] = jnp.concatenate([out_high, out_low, out_high], axis=1)
    for at, part in enumerate(split(tiled_diagonal(u_in.T, across))):
        turns[at * lanes : (at + 1) * lanes, :] = part


def scores_kernel(sources, far, tokens, which, turn, back, turns, inverse, train, *refs):
    blocks, given = refs[:sources], refs[sources : sources + (len(which) if far else 0)]
    outs, (rows, scratch) = refs[len(blocks) + len(given) : -2], refs[-2:]
    rank = turn.shape[0] // 2
    across = lanes // rank
    here = blocks[0].shape[0] // tokens
    queries = here * sources
    groups = queries // across
    back, inverse = back[...], inverse[...] * (1.0 / tokens)
    mask = (
        lax.broadcasted_iota(jnp.int32, (across * tokens, lanes), 0) // tokens
        == lax.broadcasted_iota(jnp.int32, (across * tokens, lanes), 1) // rank
    )
    parts = []
    for block in blocks:
        both = dot(block[...], turn[...])
        parts.append(split(both[:, :lanes] + both[:, lanes:]))
    scaled = []
    for group in range(groups):
        high, low = [], []
        for j in range(across):
            query = j * groups + group
            start = query % here * tokens
            for kept, part in zip((high, low), parts[query // here]):
                kept.append(part[start : start + tokens])
        high, low = jnp.concatenate(high, axis=0), jnp.concatenate(low, axis=0)
        out_high, out_low = high[:, :rank], low[:, :rank]
        in_high, in_low = (
            jnp.where(mask, jnp.concatenate([x[:, lanes // 2 :]] * 2, axis=1), jnp.zeros(mask.shape, bf16))
            for x in (high, low)
        )
        gradient = dot(
            jnp.concatenate([out_high, out_low, out_high], axis=0),
            jnp.concatenate([in_high, in_high, in_low], axis=0),
            tn,
        )
        high, low = split(gradient * inverse)
        scaled.append(dot(back, jnp.concatenate([high, high, low], axis=0)))
    scaled = jnp.concatenate(scaled, axis=0)
    conditioned = product3(scaled, turns[:lanes, :], turns[lanes:, :])
    for part in range(lanes // 128):
        scratch[part, : conditioned.shape[0], :] = conditioned[:, part * 128 : (part + 1) * 128]
    for pair in range(rank // 2):
        for part in range(lanes // 128):
            even = scratch[part, pl.ds(2 * pair, groups, stride=rank), :]
            odd = scratch[part, pl.ds(2 * pair + 1, groups, stride=rank), :]
            columns = slice(2 * pair * rank, 2 * (pair + 1) * rank)
            for half in range(2):
                j = 2 * part + half
                cut = slice(half * rank, (half + 1) * rank)
                rows[j * groups : (j + 1) * groups, columns] = jnp.concatenate(
                    [even[:, cut], odd[:, cut]], axis=1
                )
    write_slabs(far, which, here, rows, train, given, outs)


def slabs_kernel(far, which, here, rows, train, *refs):
    write_slabs(far, which, here, rows, train, refs[: len(which)], refs[len(which) :])


def write_slabs(far, which, here, rows, train, given, outs):
    layer, place = lax.axis_index("layer"), lax.axis_index("corpus")
    slab_rows = train.shape[0] // lax.axis_size("layer")
    conditioned = rows[...].astype(bf16)
    for at, shift in enumerate(which):
        if outs[at].shape[1] > slab_rows:
            outs[at][:, slab_rows:] = jnp.zeros((outs[at].shape[0], outs[at].shape[1] - slab_rows), f32)
        first = pl.multiple_of((layer ^ shift) * slab_rows, 16)
        slab = dot(train[pl.ds(first, slab_rows), :], conditioned, nt).T
        if not far:
            outs[at][...] = slab
            continue
        outs[at][pl.ds(pl.multiple_of(place * here, 8), here), :slab_rows] = given[at][...]
        for block, distance in enumerate(far):
            to = pl.ds(pl.multiple_of((place ^ distance) * here, 8), here)
            outs[at][to, :slab_rows] = slab[block * here : (block + 1) * here]


def body(
    query_acts,
    query_outgrads,
    in_project,
    out_project,
    in_basis,
    out_basis,
    eig_values,
    train_grads,
):
    queries_here, _, tokens, model = query_acts.shape
    rank, width = in_project.shape[1:]
    places = model // width
    layers = lax.axis_size("layer")
    acts = query_acts.reshape(queries_here * tokens, model)
    outgrads = query_outgrads.reshape(queries_here * tokens, model)
    in_own, out_own = in_project[0], out_project[0]

    def far(x, shift):
        return lax.ppermute(x, "corpus", [(i, i ^ shift) for i in range(places)])

    def mixed(x, shifts):
        pairs = [(g * places + i, g * places + (i ^ shifts[g])) for g in range(2) for i in range(places)]
        return lax.ppermute(x, ("groups", "corpus"), pairs)

    def swapped(x):
        return lax.ppermute(x, "groups", [(0, 1), (1, 0)])

    def sides_call(plan, pieces, totals, dtype):
        return pl.pallas_call(
            functools.partial(sides_kernel, plan),
            out_shape=jax.ShapeDtypeStruct((queries_here * tokens, 2 * rank), dtype),
            in_specs=[vmem] * (2 + len(pieces) + len(totals)),
            out_specs=vmem,
            compiler_params=params,
            name="sides",
        )(acts, outgrads, *pieces, *totals)

    stay = functools.partial(pltpu.with_memory_space_constraint, memory_space=pltpu.HBM)
    hbm = pl.BlockSpec(memory_space=pltpu.HBM)
    prepared = pl.pallas_call(
        prepare_kernel,
        out_shape=[
            jax.ShapeDtypeStruct((queries_here * tokens, 2 * rank), f32),
            jax.ShapeDtypeStruct(acts.shape, bf16),
            jax.ShapeDtypeStruct(acts.shape, bf16),
            jax.ShapeDtypeStruct((2 * rank, 2 * lanes), bf16),
            jax.ShapeDtypeStruct((rank, 3 * rank), bf16),
            jax.ShapeDtypeStruct((2 * lanes, lanes), bf16),
            jax.ShapeDtypeStruct((rank, lanes), f32),
        ],
        in_specs=[hbm] * 7,
        out_specs=[vmem] * 7,
        scratch_shapes=[
            pltpu.VMEM((rank, width), bf16),
            pltpu.VMEM((rank, width), bf16),
            pltpu.VMEM((rank, rank), f32),
            pltpu.VMEM((rank, rank), f32),
            pltpu.VMEM((1, rank * rank), f32),
            pltpu.VMEM((rank, rank), f32),
            pltpu.SemaphoreType.DMA((7,)),
        ],
        compiler_params=params,
        name="prepare",
    )(*(stay(x) for x in (in_own, out_own, acts, outgrads, in_basis[0], out_basis[0], eig_values)))
    total, acts, outgrads = prepared[:3]
    train = train_grads.reshape(train_grads.shape[0], rank * rank)
    rows_out = train.shape[0] // layers

    def slab_shapes(queries, count, wide=0):
        return [jax.ShapeDtypeStruct((queries, rows_out + wide), f32)] * count

    def scores_call(far, which, blocks, given, chunks):
        here = blocks[0].shape[0] // tokens // chunks
        count = here * len(blocks)
        queries = count * chunks + (queries_here if far else 0)
        scratch = pltpu.VMEM((lanes // 128, count * rank * rank // lanes + rank, 128), f32)
        shapes, rows = slab_shapes(queries, len(which), -rows_out % 128 if far else 0), (count, rank * rank)
        specs = dict(in_specs=[vmem] * (5 + len(blocks) + len(given)), out_specs=[vmem] * len(which))
        if chunks > 1:
            specs = dict(
                grid=(chunks,),
                in_specs=[vmem] * 5 + [pl.BlockSpec((here * tokens, 2 * rank), lambda i: (i, 0))],
                out_specs=[pl.BlockSpec((here, rows_out), lambda i: (i, 0))] * len(which),
            )
        if far:
            shapes.append(jax.ShapeDtypeStruct(rows, f32))
            specs["out_specs"].append(vmem)
            scratches = [scratch]
        else:
            scratches = [pltpu.VMEM(rows, f32), scratch]
        return pl.pallas_call(
            functools.partial(scores_kernel, len(blocks), far, tokens, which),
            out_shape=shapes,
            scratch_shapes=scratches,
            compiler_params=params,
            name="scores",
            **specs,
        )(*prepared[3:], train, *blocks, *given)

    if places == 4 and lax.axis_size("groups") == 2:
        part = width // 2
        near = mixed(in_own, (3, 1))
        near_out = mixed(out_own, (1, 3))
        last, last_out = far(in_own, 2), far(out_own, 2)
        near, total = lax.optimization_barrier((near, total))
        direct = lambda g, p: (p ^ 2) * width
        first = lambda g, p: (p ^ jnp.where(g == 0, 3, 1)) * width
        second = lambda g, p: (p ^ jnp.where(g == 0, 1, 3)) * width
        mine = lambda g, p: (p ^ 2) * width + g * part
        other = lambda g, p: (p ^ 2) * width + (1 - g) * part
        total = sides_call([(1, first), (0, second)], [near, near_out], [total], f32)
        sides = sides_call([(1, second), (0, first), (1, direct), (0, direct)], [swapped(near), swapped(near_out), last, last_out], [total], bf16)
        arrived = [far(sides, shift) for shift in (3, 2, 1)]
        own = scores_call((), tuple(range(layers)), [sides], [], 1)
        soon, later = tuple(range(layers // 2, layers)), tuple(range(layers // 2))
        *slabs, rows = scores_call((3, 2, 1), soon, arrived, [own[i] for i in soon], 1)
        slabs = pl.pallas_call(
            functools.partial(slabs_kernel, (3, 2, 1), later, queries_here),
            out_shape=slab_shapes(slabs[0].shape[0], len(later)),
            in_specs=[vmem] * (2 + len(later)),
            out_specs=[vmem] * len(later),
            compiler_params=params,
            name="slabs",
        )(rows, train, *(own[i] for i in later)) + tuple(slabs)
    else:
        pieces = [lax.all_gather(x, "corpus", axis=1, tiled=True) for x in (in_own, out_own)]
        sides = sides_call([(1, lambda g, p: 0), (0, lambda g, p: 0)], pieces, [], bf16)
        everything = lax.all_gather(sides, "corpus", axis=0, tiled=True)
        slabs = scores_call((), tuple(range(layers)), [everything], [], everything.shape[0] // tokens // 32)

    total = slabs[0]
    for shift in range(1, layers):
        total += lax.ppermute(slabs[shift], "layer", [(i, i ^ shift) for i in range(layers)])[:, :rows_out]
    return total.T


def solution(mesh):
    placed = (
        P(("groups", "corpus"), "layer", None, None),
        P(("groups", "corpus"), "layer", None, None),
        P("layer", None, "corpus"),
        P("layer", None, "corpus"),
        P("layer", None, None),
        P("layer", None, None),
        P("layer", None),
        P(("groups", "corpus"), "layer", None),
    )
    return jax.shard_map(
        body,
        mesh=mesh,
        in_specs=placed,
        out_specs=P(("groups", "corpus", "layer"), None),
        check_vma=False,
    )
```

```python
import functools

import jax
import jax.numpy as jnp
from jax import lax
from jax.experimental import pallas as pl
from jax.experimental.pallas import tpu as pltpu
from jax.sharding import PartitionSpec as P

damping = 0.1
f32 = jnp.float32
bf16 = jnp.bfloat16
lanes = 256
nt = (((1,), (1,)), ((), ()))
tn = (((0,), (0,)), ((), ()))
vmem = pl.BlockSpec(memory_space=pltpu.VMEM)
params = pltpu.CompilerParams(vmem_limit_bytes=16 << 20)


def dot(a, b, dims=(((1,), (0,)), ((), ()))):
    return lax.dot_general(a, b, dims, preferred_element_type=f32)


def split(x):
    high = x.astype(bf16)
    return high, (x - high.astype(f32)).astype(bf16)


def tiled_diagonal(x, blocks):
    n = x.shape[0]
    wide = jnp.concatenate([x] * blocks, axis=1)
    tall = jnp.concatenate([wide] * blocks, axis=0)
    row = lax.broadcasted_iota(jnp.int32, tall.shape, 0) // n
    column = lax.broadcasted_iota(jnp.int32, tall.shape, 1) // n
    return jnp.where(row == column, tall, 0.0)


def product3(x, high, low):
    x_high, x_low = split(x)
    return dot(x_high, high) + (dot(x_low, high) + dot(x_high, low))


def sides_kernel(plan, acts, outgrads, *refs):
    total, sides = refs[len(plan) : -1], refs[-1]
    group, place = lax.axis_index("groups"), lax.axis_index("corpus")
    sums = [jnp.zeros((acts.shape[0], sides.shape[1] // 2), f32)] * 2
    for (side, first), piece in zip(plan, refs):
        width = piece.shape[1]
        columns = pl.ds(pl.multiple_of(first(group, place), 128), width)
        inputs = acts if side else outgrads
        sums[side] += dot(inputs[:, columns], piece[...], nt)
    result = jnp.concatenate(sums, axis=1)
    if total:
        result += total[0][...]
    sides[...] = result.astype(sides.dtype)


def prepare_kernel(in_own, out_own, acts, outgrads, in_basis, out_basis, eigen, *refs):
    total, acts_here, outgrads_here, turn, back, turns, inverse = refs[:7]
    in_here, out_here, u_in, u_out, values, spread, sems = refs[7:]
    width = in_own.shape[1]
    pairs = [(in_basis, u_in), (out_basis, u_out), (eigen, values)]
    pairs += [(in_own, in_here), (out_own, out_here), (acts, acts_here), (outgrads, outgrads_here)]
    copies = [pltpu.make_async_copy(a, b, sems.at[i]) for i, (a, b) in enumerate(pairs)]
    for copy in copies:
        copy.start()
    for copy in copies[:3]:
        copy.wait()
    lay_out(u_in, u_out, values, turn, back, turns, inverse, spread)
    for copy in copies[3:]:
        copy.wait()
    columns = pl.ds(pl.multiple_of(lax.axis_index("corpus") * width, 128), width)
    total[...] = jnp.concatenate(
        [dot(outgrads_here[:, columns], out_here[...], nt), dot(acts_here[:, columns], in_here[...], nt)], axis=1
    )


def lay_out(in_basis, out_basis, eigen, turn, back, turns, inverse, spread):
    rank = in_basis.shape[0]
    across = lanes // rank
    for at in range(rank):
        spread[at : at + 1, :] = eigen[:, at * rank : (at + 1) * rank]
    inverse[...] = jnp.concatenate([1.0 / (spread[...] + damping)] * across, axis=1)
    out_high, out_low = split(out_basis[...])
    u_in = in_basis[...]
    in_high, in_low = split(u_in)
    for at, (of_out, of_in) in enumerate(((out_high, in_high), (out_low, in_low))):
        zero = jnp.zeros_like(of_out)
        top = jnp.concatenate([of_out, of_out, zero, zero], axis=1)
        bottom = jnp.concatenate([zero, zero, of_in, of_in], axis=1)
        turn[:, at * lanes : (at + 1) * lanes] = jnp.concatenate([top, bottom], axis=0)
    back[...] = jnp.concatenate([out_high, out_low, out_high], axis=1)
    for at, part in enumerate(split(tiled_diagonal(u_in.T, across))):
        turns[at * lanes : (at + 1) * lanes, :] = part


def scores_kernel(sources, far, tokens, which, turn, back, turns, inverse, train, *refs):
    blocks, given = refs[:sources], refs[sources : sources + (len(which) if far else 0)]
    outs, (rows, scratch) = refs[len(blocks) + len(given) : -2], refs[-2:]
    rank = turn.shape[0] // 2
    across = lanes // rank
    here = blocks[0].shape[0] // tokens
    queries = here * sources
    groups = queries // across
    back, inverse = back[...], inverse[...] * (1.0 / tokens)
    mask = (
        lax.broadcasted_iota(jnp.int32, (across * tokens, lanes), 0) // tokens
        == lax.broadcasted_iota(jnp.int32, (across * tokens, lanes), 1) // rank
    )
    parts = []
    for block in blocks:
        both = dot(block[...], turn[...])
        parts.append(split(both[:, :lanes] + both[:, lanes:]))
    scaled = []
    for group in range(groups):
        high, low = [], []
        for j in range(across):
            query = j * groups + group
            start = query % here * tokens
            for kept, part in zip((high, low), parts[query // here]):
                kept.append(part[start : start + tokens])
        high, low = jnp.concatenate(high, axis=0), jnp.concatenate(low, axis=0)
        out_high, out_low = high[:, :rank], low[:, :rank]
        in_high, in_low = (
            jnp.where(mask, jnp.concatenate([x[:, lanes // 2 :]] * 2, axis=1), jnp.zeros(mask.shape, bf16))
            for x in (high, low)
        )
        gradient = dot(
            jnp.concatenate([out_high, out_low, out_high], axis=0),
            jnp.concatenate([in_high, in_high, in_low], axis=0),
            tn,
        )
        high, low = split(gradient * inverse)
        scaled.append(dot(back, jnp.concatenate([high, high, low], axis=0)))
    scaled = jnp.concatenate(scaled, axis=0)
    conditioned = product3(scaled, turns[:lanes, :], turns[lanes:, :])
    for part in range(lanes // 128):
        scratch[part, : conditioned.shape[0], :] = conditioned[:, part * 128 : (part + 1) * 128]
    for pair in range(rank // 2):
        for part in range(lanes // 128):
            even = scratch[part, pl.ds(2 * pair, groups, stride=rank), :]
            odd = scratch[part, pl.ds(2 * pair + 1, groups, stride=rank), :]
            columns = slice(2 * pair * rank, 2 * (pair + 1) * rank)
            for half in range(2):
                j = 2 * part + half
                cut = slice(half * rank, (half + 1) * rank)
                rows[j * groups : (j + 1) * groups, columns] = jnp.concatenate(
                    [even[:, cut], odd[:, cut]], axis=1
                )
    write_slabs(far, which, here, rows, train, given, outs)


def slabs_kernel(far, which, here, rows, train, *refs):
    write_slabs(far, which, here, rows, train, refs[: len(which)], refs[len(which) :])


def write_slabs(far, which, here, rows, train, given, outs):
    layer, place = lax.axis_index("layer"), lax.axis_index("corpus")
    slab_rows = train.shape[0] // lax.axis_size("layer")
    conditioned = rows[...].astype(bf16)
    for at, shift in enumerate(which):
        if outs[at].shape[1] > slab_rows:
            outs[at][:, slab_rows:] = jnp.zeros((outs[at].shape[0], outs[at].shape[1] - slab_rows), f32)
        first = pl.multiple_of((layer ^ shift) * slab_rows, 16)
        slab = dot(train[pl.ds(first, slab_rows), :], conditioned, nt).T
        if not far:
            outs[at][...] = slab
            continue
        outs[at][pl.ds(pl.multiple_of(place * here, 8), here), :slab_rows] = given[at][...]
        for block, distance in enumerate(far):
            to = pl.ds(pl.multiple_of((place ^ distance) * here, 8), here)
            outs[at][to, :slab_rows] = slab[block * here : (block + 1) * here]


def body(
    query_acts,
    query_outgrads,
    in_project,
    out_project,
    in_basis,
    out_basis,
    eig_values,
    train_grads,
):
    queries_here, _, tokens, model = query_acts.shape
    rank, width = in_project.shape[1:]
    places = model // width
    layers = lax.axis_size("layer")
    acts = query_acts.reshape(queries_here * tokens, model)
    outgrads = query_outgrads.reshape(queries_here * tokens, model)
    in_own, out_own = in_project[0], out_project[0]

    def far(x, shift):
        return lax.ppermute(x, "corpus", [(i, i ^ shift) for i in range(places)])

    def mixed(x, shifts):
        pairs = [(g * places + i, g * places + (i ^ shifts[g])) for g in range(2) for i in range(places)]
        return lax.ppermute(x, ("groups", "corpus"), pairs)

    def swapped(x):
        return lax.ppermute(x, "groups", [(0, 1), (1, 0)])

    def sides_call(plan, pieces, totals, dtype):
        return pl.pallas_call(
            functools.partial(sides_kernel, plan),
            out_shape=jax.ShapeDtypeStruct((queries_here * tokens, 2 * rank), dtype),
            in_specs=[vmem] * (2 + len(pieces) + len(totals)),
            out_specs=vmem,
            compiler_params=params,
            name="sides",
        )(acts, outgrads, *pieces, *totals)

    stay = functools.partial(pltpu.with_memory_space_constraint, memory_space=pltpu.HBM)
    hbm = pl.BlockSpec(memory_space=pltpu.HBM)
    prepared = pl.pallas_call(
        prepare_kernel,
        out_shape=[
            jax.ShapeDtypeStruct((queries_here * tokens, 2 * rank), f32),
            jax.ShapeDtypeStruct(acts.shape, bf16),
            jax.ShapeDtypeStruct(acts.shape, bf16),
            jax.ShapeDtypeStruct((2 * rank, 2 * lanes), bf16),
            jax.ShapeDtypeStruct((rank, 3 * rank), bf16),
            jax.ShapeDtypeStruct((2 * lanes, lanes), bf16),
            jax.ShapeDtypeStruct((rank, lanes), f32),
        ],
        in_specs=[hbm] * 7,
        out_specs=[vmem] * 7,
        scratch_shapes=[
            pltpu.VMEM((rank, width), bf16),
            pltpu.VMEM((rank, width), bf16),
            pltpu.VMEM((rank, rank), f32),
            pltpu.VMEM((rank, rank), f32),
            pltpu.VMEM((1, rank * rank), f32),
            pltpu.VMEM((rank, rank), f32),
            pltpu.SemaphoreType.DMA((7,)),
        ],
        compiler_params=params,
        name="prepare",
    )(*(stay(x) for x in (in_own, out_own, acts, outgrads, in_basis[0], out_basis[0], eig_values)))
    total, acts, outgrads = prepared[:3]
    train = train_grads.reshape(train_grads.shape[0], rank * rank)
    rows_out = train.shape[0] // layers

    def slab_shapes(queries, count, wide=0):
        return [jax.ShapeDtypeStruct((queries, rows_out + wide), f32)] * count

    def scores_call(far, which, blocks, given, chunks):
        here = blocks[0].shape[0] // tokens // chunks
        count = here * len(blocks)
        queries = count * chunks + (queries_here if far else 0)
        scratch = pltpu.VMEM((lanes // 128, count * rank * rank // lanes + rank, 128), f32)
        shapes, rows = slab_shapes(queries, len(which), -rows_out % 128 if far else 0), (count, rank * rank)
        specs = dict(in_specs=[vmem] * (5 + len(blocks) + len(given)), out_specs=[vmem] * len(which))
        if chunks > 1:
            specs = dict(
                grid=(chunks,),
                in_specs=[vmem] * 5 + [pl.BlockSpec((here * tokens, 2 * rank), lambda i: (i, 0))],
                out_specs=[pl.BlockSpec((here, rows_out), lambda i: (i, 0))] * len(which),
            )
        if far:
            shapes.append(jax.ShapeDtypeStruct(rows, f32))
            specs["out_specs"].append(vmem)
            scratches = [scratch]
        else:
            scratches = [pltpu.VMEM(rows, f32), scratch]
        return pl.pallas_call(
            functools.partial(scores_kernel, len(blocks), far, tokens, which),
            out_shape=shapes,
            scratch_shapes=scratches,
            compiler_params=params,
            name="scores",
            **specs,
        )(*prepared[3:], train, *blocks, *given)

    if places == 4 and lax.axis_size("groups") == 2:
        part = width // 2
        near = mixed(in_own, (3, 1))
        near_out = mixed(out_own, (1, 3))
        last, last_out = far(in_own, 2), far(out_own, 2)
        near, total = lax.optimization_barrier((near, total))
        direct = lambda g, p: (p ^ 2) * width
        first = lambda g, p: (p ^ jnp.where(g == 0, 3, 1)) * width
        second = lambda g, p: (p ^ jnp.where(g == 0, 1, 3)) * width
        mine = lambda g, p: (p ^ 2) * width + g * part
        other = lambda g, p: (p ^ 2) * width + (1 - g) * part
        total = sides_call([(1, first), (0, second), (1, direct)], [near, near_out, last], [total], f32)
        sides = sides_call(
            [(1, second), (0, first), (0, direct)], [swapped(near), swapped(near_out), last_out], [total], bf16
        )
        arrived = [far(sides, shift) for shift in (3, 2, 1)]
        own = scores_call((), tuple(range(layers)), [sides], [], 1)
        soon, later = tuple(range(layers // 2, layers)), tuple(range(layers // 2))
        *slabs, rows = scores_call((3, 2, 1), soon, arrived, [own[i] for i in soon], 1)
        slabs = pl.pallas_call(
            functools.partial(slabs_kernel, (3, 2, 1), later, queries_here),
            out_shape=slab_shapes(slabs[0].shape[0], len(later)),
            in_specs=[vmem] * (2 + len(later)),
            out_specs=[vmem] * len(later),
            compiler_params=params,
            name="slabs",
        )(rows, train, *(own[i] for i in later)) + tuple(slabs)
    else:
        pieces = [lax.all_gather(x, "corpus", axis=1, tiled=True) for x in (in_own, out_own)]
        sides = sides_call([(1, lambda g, p: 0), (0, lambda g, p: 0)], pieces, [], bf16)
        everything = lax.all_gather(sides, "corpus", axis=0, tiled=True)
        slabs = scores_call((), tuple(range(layers)), [everything], [], everything.shape[0] // tokens // 32)

    total = slabs[0]
    for shift in range(1, layers):
        total += lax.ppermute(slabs[shift], "layer", [(i, i ^ shift) for i in range(layers)])[:, :rows_out]
    return total.T


def solution(mesh):
    placed = (
        P(("groups", "corpus"), "layer", None, None),
        P(("groups", "corpus"), "layer", None, None),
        P("layer", None, "corpus"),
        P("layer", None, "corpus"),
        P("layer", None, None),
        P("layer", None, None),
        P("layer", None),
        P(("groups", "corpus"), "layer", None),
    )
    return jax.shard_map(
        body,
        mesh=mesh,
        in_specs=placed,
        out_specs=P(("groups", "corpus", "layer"), None),
        check_vma=False,
    )
```

```python
import functools

import jax
import jax.numpy as jnp
from jax import lax
from jax.experimental import pallas as pl
from jax.experimental.pallas import tpu as pltpu
from jax.sharding import PartitionSpec as P

damping = 0.1
f32 = jnp.float32
bf16 = jnp.bfloat16
lanes = 256
nt = (((1,), (1,)), ((), ()))
tn = (((0,), (0,)), ((), ()))
vmem = pl.BlockSpec(memory_space=pltpu.VMEM)
params = pltpu.CompilerParams(vmem_limit_bytes=16 << 20)


def dot(a, b, dims=(((1,), (0,)), ((), ()))):
    return lax.dot_general(a, b, dims, preferred_element_type=f32)


def split(x):
    high = x.astype(bf16)
    return high, (x - high.astype(f32)).astype(bf16)


def tiled_diagonal(x, blocks):
    n = x.shape[0]
    wide = jnp.concatenate([x] * blocks, axis=1)
    tall = jnp.concatenate([wide] * blocks, axis=0)
    row = lax.broadcasted_iota(jnp.int32, tall.shape, 0) // n
    column = lax.broadcasted_iota(jnp.int32, tall.shape, 1) // n
    return jnp.where(row == column, tall, 0.0)


def product3(x, high, low):
    x_high, x_low = split(x)
    return dot(x_high, high) + (dot(x_low, high) + dot(x_high, low))


def sides_kernel(plan, acts, outgrads, *refs):
    total, sides = refs[len(plan) : -1], refs[-1]
    group, place = lax.axis_index("groups"), lax.axis_index("corpus")
    sums = [jnp.zeros((acts.shape[0], sides.shape[1] // 2), f32)] * 2
    for (side, first), piece in zip(plan, refs):
        width = piece.shape[1]
        columns = pl.ds(pl.multiple_of(first(group, place), 128), width)
        inputs = acts if side else outgrads
        sums[side] += dot(inputs[:, columns], piece[...], nt)
    result = jnp.concatenate(sums, axis=1)
    if total:
        result += total[0][...]
    sides[...] = result.astype(sides.dtype)


def prepare_kernel(in_own, out_own, acts, outgrads, in_basis, out_basis, eigen, *refs):
    total, acts_here, outgrads_here, turn, back, turns, inverse = refs[:7]
    in_here, out_here, u_in, u_out, values, spread, sems = refs[7:]
    width = in_own.shape[1]
    pairs = [(in_basis, u_in), (out_basis, u_out), (eigen, values)]
    pairs += [(in_own, in_here), (out_own, out_here), (acts, acts_here), (outgrads, outgrads_here)]
    copies = [pltpu.make_async_copy(a, b, sems.at[i]) for i, (a, b) in enumerate(pairs)]
    for copy in copies:
        copy.start()
    for copy in copies[:3]:
        copy.wait()
    lay_out(u_in, u_out, values, turn, back, turns, inverse, spread)
    for copy in copies[3:]:
        copy.wait()
    columns = pl.ds(pl.multiple_of(lax.axis_index("corpus") * width, 128), width)
    total[...] = jnp.concatenate(
        [dot(outgrads_here[:, columns], out_here[...], nt), dot(acts_here[:, columns], in_here[...], nt)], axis=1
    )


def lay_out(in_basis, out_basis, eigen, turn, back, turns, inverse, spread):
    rank = in_basis.shape[0]
    across = lanes // rank
    for at in range(rank):
        spread[at : at + 1, :] = eigen[:, at * rank : (at + 1) * rank]
    inverse[...] = jnp.concatenate([1.0 / (spread[...] + damping)] * across, axis=1)
    out_high, out_low = split(out_basis[...])
    u_in = in_basis[...]
    in_high, in_low = split(u_in)
    for at, (of_out, of_in) in enumerate(((out_high, in_high), (out_low, in_low))):
        zero = jnp.zeros_like(of_out)
        top = jnp.concatenate([of_out, zero], axis=1)
        bottom = jnp.concatenate([zero, of_in], axis=1)
        turn[:, at * 2 * rank : (at + 1) * 2 * rank] = jnp.concatenate([top, bottom], axis=0)
    back[...] = jnp.concatenate([out_high, out_low, out_high], axis=1)
    for at, part in enumerate(split(tiled_diagonal(u_in.T, across))):
        turns[at * lanes : (at + 1) * lanes, :] = part


def scores_kernel(sources, far, tokens, which, turn, back, turns, inverse, train, *refs):
    blocks, given = refs[:sources], refs[sources : sources + (len(which) if far else 0)]
    outs, (rows, scratch) = refs[len(blocks) + len(given) : -2], refs[-2:]
    rank = turn.shape[0] // 2
    across = lanes // rank
    here = blocks[0].shape[0] // tokens
    queries = here * sources
    groups = queries // across
    back, inverse = back[...], inverse[...] * (1.0 / tokens)
    mask = (
        lax.broadcasted_iota(jnp.int32, (across * tokens, lanes), 0) // tokens
        == lax.broadcasted_iota(jnp.int32, (across * tokens, lanes), 1) // rank
    )
    parts = []
    for block in blocks:
        both = dot(block[...], turn[...])
        parts.append(split(both[:, : 2 * rank] + both[:, 2 * rank :]))
    scaled = []
    for group in range(groups):
        high, low = [], []
        for j in range(across):
            query = j * groups + group
            start = query % here * tokens
            for kept, part in zip((high, low), parts[query // here]):
                kept.append(part[start : start + tokens])
        high, low = jnp.concatenate(high, axis=0), jnp.concatenate(low, axis=0)
        out_high, out_low = high[:, :rank], low[:, :rank]
        in_high, in_low = (
            jnp.where(mask, jnp.concatenate([x[:, rank:]] * across, axis=1), jnp.zeros(mask.shape, bf16))
            for x in (high, low)
        )
        gradient = dot(
            jnp.concatenate([out_high, out_low, out_high], axis=0),
            jnp.concatenate([in_high, in_high, in_low], axis=0),
            tn,
        )
        high, low = split(gradient * inverse)
        scaled.append(dot(back, jnp.concatenate([high, high, low], axis=0)))
    scaled = jnp.concatenate(scaled, axis=0)
    conditioned = product3(scaled, turns[:lanes, :], turns[lanes:, :])
    for part in range(lanes // 128):
        scratch[part, : conditioned.shape[0], :] = conditioned[:, part * 128 : (part + 1) * 128]
    for pair in range(rank // 2):
        for part in range(lanes // 128):
            even = scratch[part, pl.ds(2 * pair, groups, stride=rank), :]
            odd = scratch[part, pl.ds(2 * pair + 1, groups, stride=rank), :]
            columns = slice(2 * pair * rank, 2 * (pair + 1) * rank)
            for half in range(2):
                j = 2 * part + half
                cut = slice(half * rank, (half + 1) * rank)
                rows[j * groups : (j + 1) * groups, columns] = jnp.concatenate(
                    [even[:, cut], odd[:, cut]], axis=1
                )
    write_slabs(far, which, here, rows, train, given, outs)


def slabs_kernel(far, which, here, rows, train, *refs):
    write_slabs(far, which, here, rows, train, refs[: len(which)], refs[len(which) :])


def write_slabs(far, which, here, rows, train, given, outs):
    layer, place = lax.axis_index("layer"), lax.axis_index("corpus")
    slab_rows = train.shape[0] // lax.axis_size("layer")
    conditioned = rows[...].astype(bf16)
    for at, shift in enumerate(which):
        if outs[at].shape[1] > slab_rows:
            outs[at][:, slab_rows:] = jnp.zeros((outs[at].shape[0], outs[at].shape[1] - slab_rows), f32)
        first = pl.multiple_of((layer ^ shift) * slab_rows, 16)
        slab = dot(train[pl.ds(first, slab_rows), :], conditioned, nt).T
        if not far:
            outs[at][...] = slab
            continue
        outs[at][pl.ds(pl.multiple_of(place * here, 8), here), :slab_rows] = given[at][...]
        for block, distance in enumerate(far):
            to = pl.ds(pl.multiple_of((place ^ distance) * here, 8), here)
            outs[at][to, :slab_rows] = slab[block * here : (block + 1) * here]


def body(
    query_acts,
    query_outgrads,
    in_project,
    out_project,
    in_basis,
    out_basis,
    eig_values,
    train_grads,
):
    queries_here, _, tokens, model = query_acts.shape
    rank, width = in_project.shape[1:]
    places = model // width
    layers = lax.axis_size("layer")
    acts = query_acts.reshape(queries_here * tokens, model)
    outgrads = query_outgrads.reshape(queries_here * tokens, model)
    in_own, out_own = in_project[0], out_project[0]

    def far(x, shift):
        return lax.ppermute(x, "corpus", [(i, i ^ shift) for i in range(places)])

    def mixed(x, shifts):
        pairs = [(g * places + i, g * places + (i ^ shifts[g])) for g in range(2) for i in range(places)]
        return lax.ppermute(x, ("groups", "corpus"), pairs)

    def swapped(x):
        return lax.ppermute(x, "groups", [(0, 1), (1, 0)])

    def sides_call(plan, pieces, totals, dtype):
        return pl.pallas_call(
            functools.partial(sides_kernel, plan),
            out_shape=jax.ShapeDtypeStruct((queries_here * tokens, 2 * rank), dtype),
            in_specs=[vmem] * (2 + len(pieces) + len(totals)),
            out_specs=vmem,
            compiler_params=params,
            name="sides",
        )(acts, outgrads, *pieces, *totals)

    stay = functools.partial(pltpu.with_memory_space_constraint, memory_space=pltpu.HBM)
    hbm = pl.BlockSpec(memory_space=pltpu.HBM)
    prepared = pl.pallas_call(
        prepare_kernel,
        out_shape=[
            jax.ShapeDtypeStruct((queries_here * tokens, 2 * rank), f32),
            jax.ShapeDtypeStruct(acts.shape, bf16),
            jax.ShapeDtypeStruct(acts.shape, bf16),
            jax.ShapeDtypeStruct((2 * rank, 4 * rank), bf16),
            jax.ShapeDtypeStruct((rank, 3 * rank), bf16),
            jax.ShapeDtypeStruct((2 * lanes, lanes), bf16),
            jax.ShapeDtypeStruct((rank, lanes), f32),
        ],
        in_specs=[hbm] * 7,
        out_specs=[vmem] * 7,
        scratch_shapes=[
            pltpu.VMEM((rank, width), bf16),
            pltpu.VMEM((rank, width), bf16),
            pltpu.VMEM((rank, rank), f32),
            pltpu.VMEM((rank, rank), f32),
            pltpu.VMEM((1, rank * rank), f32),
            pltpu.VMEM((rank, rank), f32),
            pltpu.SemaphoreType.DMA((7,)),
        ],
        compiler_params=params,
        name="prepare",
    )(*(stay(x) for x in (in_own, out_own, acts, outgrads, in_basis[0], out_basis[0], eig_values)))
    total, acts, outgrads = prepared[:3]
    train = train_grads.reshape(train_grads.shape[0], rank * rank)
    rows_out = train.shape[0] // layers

    def slab_shapes(queries, count, wide=0):
        return [jax.ShapeDtypeStruct((queries, rows_out + wide), f32)] * count

    def scores_call(far, which, blocks, given, chunks):
        here = blocks[0].shape[0] // tokens // chunks
        count = here * len(blocks)
        queries = count * chunks + (queries_here if far else 0)
        scratch = pltpu.VMEM((lanes // 128, count * rank * rank // lanes + rank, 128), f32)
        shapes, rows = slab_shapes(queries, len(which), -rows_out % 128 if far else 0), (count, rank * rank)
        specs = dict(in_specs=[vmem] * (5 + len(blocks) + len(given)), out_specs=[vmem] * len(which))
        if chunks > 1:
            specs = dict(
                grid=(chunks,),
                in_specs=[vmem] * 5 + [pl.BlockSpec((here * tokens, 2 * rank), lambda i: (i, 0))],
                out_specs=[pl.BlockSpec((here, rows_out), lambda i: (i, 0))] * len(which),
            )
        if far:
            shapes.append(jax.ShapeDtypeStruct(rows, f32))
            specs["out_specs"].append(vmem)
            scratches = [scratch]
        else:
            scratches = [pltpu.VMEM(rows, f32), scratch]
        return pl.pallas_call(
            functools.partial(scores_kernel, len(blocks), far, tokens, which),
            out_shape=shapes,
            scratch_shapes=scratches,
            compiler_params=params,
            name="scores",
            **specs,
        )(*prepared[3:], train, *blocks, *given)

    if places == 4 and lax.axis_size("groups") == 2:
        part = width // 2
        near = mixed(in_own, (3, 1))
        near_out = mixed(out_own, (1, 3))
        last, last_out = far(in_own, 2), far(out_own, 2)
        near, total = lax.optimization_barrier((near, total))
        direct = lambda g, p: (p ^ 2) * width
        first = lambda g, p: (p ^ jnp.where(g == 0, 3, 1)) * width
        second = lambda g, p: (p ^ jnp.where(g == 0, 1, 3)) * width
        mine = lambda g, p: (p ^ 2) * width + g * part
        other = lambda g, p: (p ^ 2) * width + (1 - g) * part
        total = sides_call([(1, first), (0, second), (1, direct)], [near, near_out, last], [total], f32)
        sides = sides_call(
            [(1, second), (0, first), (0, direct)], [swapped(near), swapped(near_out), last_out], [total], bf16
        )
        arrived = [far(sides, shift) for shift in (3, 2, 1)]
        own = scores_call((), tuple(range(layers)), [sides], [], 1)
        soon, later = tuple(range(layers // 2, layers)), tuple(range(layers // 2))
        *slabs, rows = scores_call((3, 2, 1), soon, arrived, [own[i] for i in soon], 1)
        slabs = pl.pallas_call(
            functools.partial(slabs_kernel, (3, 2, 1), later, queries_here),
            out_shape=slab_shapes(slabs[0].shape[0], len(later)),
            in_specs=[vmem] * (2 + len(later)),
            out_specs=[vmem] * len(later),
            compiler_params=params,
            name="slabs",
        )(rows, train, *(own[i] for i in later)) + tuple(slabs)
    else:
        pieces = [lax.all_gather(x, "corpus", axis=1, tiled=True) for x in (in_own, out_own)]
        sides = sides_call([(1, lambda g, p: 0), (0, lambda g, p: 0)], pieces, [], bf16)
        everything = lax.all_gather(sides, "corpus", axis=0, tiled=True)
        slabs = scores_call((), tuple(range(layers)), [everything], [], everything.shape[0] // tokens // 32)

    total = slabs[0]
    for shift in range(1, layers):
        total += lax.ppermute(slabs[shift], "layer", [(i, i ^ shift) for i in range(layers)])[:, :rows_out]
    return total.T


def solution(mesh):
    placed = (
        P(("groups", "corpus"), "layer", None, None),
        P(("groups", "corpus"), "layer", None, None),
        P("layer", None, "corpus"),
        P("layer", None, "corpus"),
        P("layer", None, None),
        P("layer", None, None),
        P("layer", None),
        P(("groups", "corpus"), "layer", None),
    )
    return jax.shard_map(
        body,
        mesh=mesh,
        in_specs=placed,
        out_specs=P(("groups", "corpus", "layer"), None),
        check_vma=False,
    )
```

```python
import functools

import jax
import jax.numpy as jnp
from jax import lax
from jax.experimental import pallas as pl
from jax.experimental.pallas import tpu as pltpu
from jax.sharding import PartitionSpec as P

damping = 0.1
f32 = jnp.float32
bf16 = jnp.bfloat16
lanes = 256
nt = (((1,), (1,)), ((), ()))
tn = (((0,), (0,)), ((), ()))
vmem = pl.BlockSpec(memory_space=pltpu.VMEM)
params = pltpu.CompilerParams(vmem_limit_bytes=16 << 20)


def dot(a, b, dims=(((1,), (0,)), ((), ()))):
    return lax.dot_general(a, b, dims, preferred_element_type=f32)


def split(x):
    high = x.astype(bf16)
    return high, (x - high.astype(f32)).astype(bf16)


def tiled_diagonal(x, blocks):
    n = x.shape[0]
    wide = jnp.concatenate([x] * blocks, axis=1)
    tall = jnp.concatenate([wide] * blocks, axis=0)
    row = lax.broadcasted_iota(jnp.int32, tall.shape, 0) // n
    column = lax.broadcasted_iota(jnp.int32, tall.shape, 1) // n
    return jnp.where(row == column, tall, 0.0)


def product3(x, high, low):
    x_high, x_low = split(x)
    return dot(x_high, high) + (dot(x_low, high) + dot(x_high, low))


def sides_kernel(plan, acts, outgrads, *refs):
    total, sides = refs[len(plan) : -1], refs[-1]
    group, place = lax.axis_index("groups"), lax.axis_index("corpus")
    sums = [jnp.zeros((acts.shape[0], sides.shape[1] // 2), f32)] * 2
    for (side, first), piece in zip(plan, refs):
        width = piece.shape[1]
        columns = pl.ds(pl.multiple_of(first(group, place), 128), width)
        inputs = acts if side else outgrads
        sums[side] += dot(inputs[:, columns], piece[...], nt)
    result = jnp.concatenate(sums, axis=1)
    if total:
        result += total[0][...]
    sides[...] = result.astype(sides.dtype)


def prepare_kernel(in_own, out_own, acts, outgrads, in_basis, out_basis, eigen, *refs):
    total, acts_here, outgrads_here, turn, back, turns, inverse = refs[:7]
    in_here, out_here, u_in, u_out, values, spread, sems = refs[7:]
    width = in_own.shape[1]
    pairs = [(in_basis, u_in), (out_basis, u_out), (eigen, values)]
    pairs += [(in_own, in_here), (out_own, out_here), (acts, acts_here), (outgrads, outgrads_here)]
    copies = [pltpu.make_async_copy(a, b, sems.at[i]) for i, (a, b) in enumerate(pairs)]
    for copy in copies:
        copy.start()
    for copy in copies[:3]:
        copy.wait()
    lay_out(u_in, u_out, values, turn, back, turns, inverse, spread)
    for copy in copies[3:]:
        copy.wait()
    columns = pl.ds(pl.multiple_of(lax.axis_index("corpus") * width, 128), width)
    total[...] = jnp.concatenate(
        [dot(outgrads_here[:, columns], out_here[...], nt), dot(acts_here[:, columns], in_here[...], nt)], axis=1
    )


def lay_out(in_basis, out_basis, eigen, turn, back, turns, inverse, spread):
    rank = in_basis.shape[0]
    across = lanes // rank
    for at in range(rank):
        spread[at : at + 1, :] = eigen[:, at * rank : (at + 1) * rank]
    inverse[...] = jnp.concatenate([1.0 / (spread[...] + damping)] * across, axis=1)
    out_high, out_low = split(out_basis[...])
    u_in = in_basis[...]
    in_high, in_low = split(u_in)
    for at, (of_out, of_in) in enumerate(((out_high, in_high), (out_low, in_low))):
        zero = jnp.zeros_like(of_out)
        top = jnp.concatenate([of_out, zero], axis=1)
        bottom = jnp.concatenate([zero, of_in], axis=1)
        turn[:, at * 2 * rank : (at + 1) * 2 * rank] = jnp.concatenate([top, bottom], axis=0)
    back[...] = jnp.concatenate([out_high, out_low, out_high], axis=1)
    for at, part in enumerate(split(tiled_diagonal(u_in.T, across))):
        turns[at * lanes : (at + 1) * lanes, :] = part


def scores_kernel(sources, far, tokens, which, turn, back, turns, inverse, train, *refs):
    blocks, given = refs[:sources], refs[sources : sources + (len(which) if far else 0)]
    outs, (rows, scratch) = refs[len(blocks) + len(given) : -2], refs[-2:]
    rank = turn.shape[0] // 2
    across = lanes // rank
    here = blocks[0].shape[0] // tokens
    queries = here * sources
    groups = queries // across
    back, inverse = back[...], inverse[...] * (1.0 / tokens)
    mask = (
        lax.broadcasted_iota(jnp.int32, (across * tokens, lanes), 0) // tokens
        == lax.broadcasted_iota(jnp.int32, (across * tokens, lanes), 1) // rank
    )
    parts = []
    for block in blocks:
        both = dot(block[...], turn[...])
        parts.append(split(both[:, : 2 * rank] + both[:, 2 * rank :]))
    scaled = []
    for group in range(groups):
        high, low = [], []
        for j in range(across):
            query = j * groups + group
            start = query % here * tokens
            for kept, part in zip((high, low), parts[query // here]):
                kept.append(part[start : start + tokens])
        high, low = jnp.concatenate(high, axis=0), jnp.concatenate(low, axis=0)
        out_high, out_low = high[:, :rank], low[:, :rank]
        in_high, in_low = (
            jnp.where(mask, jnp.concatenate([x[:, rank:]] * across, axis=1), jnp.zeros(mask.shape, bf16))
            for x in (high, low)
        )
        gradient = dot(
            jnp.concatenate([out_high, out_low, out_high], axis=0),
            jnp.concatenate([in_high, in_high, in_low], axis=0),
            tn,
        )
        high, low = split(gradient * inverse)
        scaled.append(dot(back, jnp.concatenate([high, high, low], axis=0)))
    scaled = jnp.concatenate(scaled, axis=0)
    conditioned = product3(scaled, turns[:lanes, :], turns[lanes:, :])
    for part in range(lanes // 128):
        scratch[part, : conditioned.shape[0], :] = conditioned[:, part * 128 : (part + 1) * 128]
    for pair in range(rank // 2):
        for part in range(lanes // 128):
            even = scratch[part, pl.ds(2 * pair, groups, stride=rank), :]
            odd = scratch[part, pl.ds(2 * pair + 1, groups, stride=rank), :]
            columns = slice(2 * pair * rank, 2 * (pair + 1) * rank)
            for half in range(2):
                j = 2 * part + half
                cut = slice(half * rank, (half + 1) * rank)
                rows[j * groups : (j + 1) * groups, columns] = jnp.concatenate(
                    [even[:, cut], odd[:, cut]], axis=1
                )
    write_slabs(far, which, here, rows, train, given, outs)


def slabs_kernel(far, which, here, rows, train, *refs):
    write_slabs(far, which, here, rows, train, refs[: len(which)], refs[len(which) :])


def write_slabs(far, which, here, rows, train, given, outs):
    layer, place = lax.axis_index("layer"), lax.axis_index("corpus")
    slab_rows = train.shape[0] // lax.axis_size("layer")
    conditioned = rows[...].astype(bf16)
    for at, shift in enumerate(which):
        if outs[at].shape[1] > slab_rows:
            outs[at][:, slab_rows:] = jnp.zeros((outs[at].shape[0], outs[at].shape[1] - slab_rows), f32)
        first = pl.multiple_of((layer ^ shift) * slab_rows, 16)
        slab = dot(train[pl.ds(first, slab_rows), :], conditioned, nt).T
        if not far:
            outs[at][...] = slab
            continue
        outs[at][pl.ds(pl.multiple_of(place * here, 8), here), :slab_rows] = given[at][...]
        for block, distance in enumerate(far):
            to = pl.ds(pl.multiple_of((place ^ distance) * here, 8), here)
            outs[at][to, :slab_rows] = slab[block * here : (block + 1) * here]


def body(
    query_acts,
    query_outgrads,
    in_project,
    out_project,
    in_basis,
    out_basis,
    eig_values,
    train_grads,
):
    queries_here, _, tokens, model = query_acts.shape
    rank, width = in_project.shape[1:]
    places = model // width
    layers = lax.axis_size("layer")
    acts = query_acts.reshape(queries_here * tokens, model)
    outgrads = query_outgrads.reshape(queries_here * tokens, model)
    in_own, out_own = in_project[0], out_project[0]

    def far(x, shift):
        return lax.ppermute(x, "corpus", [(i, i ^ shift) for i in range(places)])

    def mixed(x, shifts):
        pairs = [(g * places + i, g * places + (i ^ shifts[g])) for g in range(2) for i in range(places)]
        return lax.ppermute(x, ("groups", "corpus"), pairs)

    def swapped(x):
        return lax.ppermute(x, "groups", [(0, 1), (1, 0)])

    def sides_call(plan, pieces, totals, dtype):
        return pl.pallas_call(
            functools.partial(sides_kernel, plan),
            out_shape=jax.ShapeDtypeStruct((queries_here * tokens, 2 * rank), dtype),
            in_specs=[vmem] * (2 + len(pieces) + len(totals)),
            out_specs=vmem,
            compiler_params=params,
            name="sides",
        )(acts, outgrads, *pieces, *totals)

    stay = functools.partial(pltpu.with_memory_space_constraint, memory_space=pltpu.HBM)
    hbm = pl.BlockSpec(memory_space=pltpu.HBM)
    prepared = pl.pallas_call(
        prepare_kernel,
        out_shape=[
            jax.ShapeDtypeStruct((queries_here * tokens, 2 * rank), f32),
            jax.ShapeDtypeStruct(acts.shape, bf16),
            jax.ShapeDtypeStruct(acts.shape, bf16),
            jax.ShapeDtypeStruct((2 * rank, 4 * rank), bf16),
            jax.ShapeDtypeStruct((rank, 3 * rank), bf16),
            jax.ShapeDtypeStruct((2 * lanes, lanes), bf16),
            jax.ShapeDtypeStruct((rank, lanes), f32),
        ],
        in_specs=[hbm] * 7,
        out_specs=[vmem] * 7,
        scratch_shapes=[
            pltpu.VMEM((rank, width), bf16),
            pltpu.VMEM((rank, width), bf16),
            pltpu.VMEM((rank, rank), f32),
            pltpu.VMEM((rank, rank), f32),
            pltpu.VMEM((1, rank * rank), f32),
            pltpu.VMEM((rank, rank), f32),
            pltpu.SemaphoreType.DMA((7,)),
        ],
        compiler_params=params,
        name="prepare",
    )(*(stay(x) for x in (in_own, out_own, acts, outgrads, in_basis[0], out_basis[0], eig_values)))
    total, acts, outgrads = prepared[:3]
    train = train_grads.reshape(train_grads.shape[0], rank * rank)
    rows_out = train.shape[0] // layers

    def slab_shapes(queries, count, wide=0):
        return [jax.ShapeDtypeStruct((queries, rows_out + wide), f32)] * count

    def scores_call(far, which, blocks, given, chunks):
        here = blocks[0].shape[0] // tokens // chunks
        count = here * len(blocks)
        queries = count * chunks + (queries_here if far else 0)
        scratch = pltpu.VMEM((lanes // 128, count * rank * rank // lanes + rank, 128), f32)
        shapes, rows = slab_shapes(queries, len(which), -rows_out % 128 if far else 0), (count, rank * rank)
        specs = dict(in_specs=[vmem] * (5 + len(blocks) + len(given)), out_specs=[vmem] * len(which))
        if chunks > 1:
            specs = dict(
                grid=(chunks,),
                in_specs=[vmem] * 5 + [pl.BlockSpec((here * tokens, 2 * rank), lambda i: (i, 0))],
                out_specs=[pl.BlockSpec((here, rows_out), lambda i: (i, 0))] * len(which),
            )
        if far:
            shapes.append(jax.ShapeDtypeStruct(rows, f32))
            specs["out_specs"].append(vmem)
            scratches = [scratch]
        else:
            scratches = [pltpu.VMEM(rows, f32), scratch]
        return pl.pallas_call(
            functools.partial(scores_kernel, len(blocks), far, tokens, which),
            out_shape=shapes,
            scratch_shapes=scratches,
            compiler_params=params,
            name="scores",
            **specs,
        )(*prepared[3:], train, *blocks, *given)

    if places == 4 and lax.axis_size("groups") == 2:
        part = width // 2
        near = mixed(in_own, (3, 1))
        near_out = mixed(out_own, (1, 3))
        last, last_out = far(in_own, 2), far(out_own, 2)
        near, total = lax.optimization_barrier((near, total))
        direct = lambda g, p: (p ^ 2) * width
        first = lambda g, p: (p ^ jnp.where(g == 0, 3, 1)) * width
        second = lambda g, p: (p ^ jnp.where(g == 0, 1, 3)) * width
        mine = lambda g, p: (p ^ 2) * width + g * part
        other = lambda g, p: (p ^ 2) * width + (1 - g) * part
        total = sides_call(
            [(1, first), (0, second), (1, direct), (1, second)], [near, near_out, last, swapped(near)], [total], f32
        )
        sides = sides_call([(0, first), (0, direct)], [swapped(near_out), last_out], [total], bf16)
        arrived = [far(sides, shift) for shift in (3, 2, 1)]
        own = scores_call((), tuple(range(layers)), [sides], [], 1)
        soon, later = tuple(range(layers // 2, layers)), tuple(range(layers // 2))
        *slabs, rows = scores_call((3, 2, 1), soon, arrived, [own[i] for i in soon], 1)
        slabs = pl.pallas_call(
            functools.partial(slabs_kernel, (3, 2, 1), later, queries_here),
            out_shape=slab_shapes(slabs[0].shape[0], len(later)),
            in_specs=[vmem] * (2 + len(later)),
            out_specs=[vmem] * len(later),
            compiler_params=params,
            name="slabs",
        )(rows, train, *(own[i] for i in later)) + tuple(slabs)
    else:
        pieces = [lax.all_gather(x, "corpus", axis=1, tiled=True) for x in (in_own, out_own)]
        sides = sides_call([(1, lambda g, p: 0), (0, lambda g, p: 0)], pieces, [], bf16)
        everything = lax.all_gather(sides, "corpus", axis=0, tiled=True)
        slabs = scores_call((), tuple(range(layers)), [everything], [], everything.shape[0] // tokens // 32)

    total = slabs[0]
    for shift in range(1, layers):
        total += lax.ppermute(slabs[shift], "layer", [(i, i ^ shift) for i in range(layers)])[:, :rows_out]
    return total.T


def solution(mesh):
    placed = (
        P(("groups", "corpus"), "layer", None, None),
        P(("groups", "corpus"), "layer", None, None),
        P("layer", None, "corpus"),
        P("layer", None, "corpus"),
        P("layer", None, None),
        P("layer", None, None),
        P("layer", None),
        P(("groups", "corpus"), "layer", None),
    )
    return jax.shard_map(
        body,
        mesh=mesh,
        in_specs=placed,
        out_specs=P(("groups", "corpus", "layer"), None),
        check_vma=False,
    )
```
